32 devices in a mesh: judge: 4 (over y, core), fsdp: 8 (over z, x).
Axes of the slice: x: 2, y: 2, z: 4, core: 2. Of those that a mesh axis runs over, the one named last changes fastest.
Arguments:
- hidden: bfloat16 [4, 8192, 4096], P('judge', 'fsdp'), may hold values from -32 to 32
- lengths: int32 [16], replicated, may hold values from 128 to 512
- duplicate_group_index: int32 [16], replicated, may hold values from 0 to 3, as said below
- attn_gain: bfloat16 [4, 4096], P('judge', 'fsdp'), may hold values from 0.5 to 1.5
- w_query: bfloat16 [4, 4096, 4096], P('judge', None, 'fsdp'), may hold values from -1 to 1
- w_key: bfloat16 [4, 4096, 1024], P('judge', 'fsdp'), may hold values from -1 to 1
- w_value: bfloat16 [4, 4096, 1024], P('judge', 'fsdp'), may hold values from -0.09375 to 0.09375
- w_out: bfloat16 [4, 4096, 4096], P('judge', 'fsdp'), may hold values from -0.09375 to 0.09375
- mlp_gain: bfloat16 [4, 4096], P('judge', 'fsdp'), may hold values from 0.5 to 1.5
- w_gate: bfloat16 [4, 4096, 14336], P('judge', None, 'fsdp'), may hold values from -0.09375 to 0.09375
- w_up: bfloat16 [4, 4096, 14336], P('judge', None, 'fsdp'), may hold values from -0.09375 to 0.09375
- w_down: bfloat16 [4, 14336, 4096], P('judge', 'fsdp'), may hold values from -0.046875 to 0.046875
- final_gain: bfloat16 [4, 4096], P('judge', 'fsdp'), may hold values from 0.5 to 1.5
- reward_head: float32 [4, 4096], P('judge'), may hold values from -8 to 8
Outputs:
- survivor_weights: float32 [16], replicated
- cluster_features: float32 [4, 4096], P(None, 'fsdp')
The draws below stay inside these ranges and needn't reach their ends.
Inputs may be any that keep to these rules, and one draw needn't show every extreme that they name: `duplicate_group_index`: every cluster holds exactly four candidates.
All inputs are finite; a program needn't handle non-finite values.
Results may differ from the reference program's by a relative error of at most 0.003.
Values may be sent and summed in bfloat16 or wider, within the bound.
A program may use at most 192 MiB of HBM per device.

```python
import math
import jax
import jax.numpy as jnp
from jax import lax

D = 4096
HEADS = 32
KV_HEADS = 8
HEAD_DIM = 128
FF = 14336
LEN = 512
JUDGES = 4
CANDS = 16
TOKENS = 8192
DUPLICATE_GROUPS = 4
KVW = 1024
N_JUDGE = 4


def column_profile(ratio):
    position = jnp.arange(D, dtype=jnp.float32) / (D - 1)
    return jnp.exp(math.log(ratio) * (position - 0.5))


def cluster_law(key):
    shuffled = jax.random.permutation(jax.random.fold_in(key, 101), CANDS)
    return (shuffled % DUPLICATE_GROUPS).astype(jnp.int32)


def draw_duplicate_group_index(key, part):
    return cluster_law(key)


def draw_hidden(key, part):
    base_noise = jax.random.truncated_normal(jax.random.fold_in(key, 1), -4.5, 4.5, (JUDGES, TOKENS, D), jnp.float32)
    values = base_noise * column_profile(10.0)[None, None, :]
    return values.astype(jnp.bfloat16)


def draw_w_query(key, part):
    matrix = jax.random.truncated_normal(jax.random.fold_in(key, 11), -4.0, 4.0, (JUDGES, D, D), jnp.float32) / math.sqrt(D)
    return matrix.astype(jnp.bfloat16)


def draw_w_key(key, part):
    matrix = jax.random.truncated_normal(jax.random.fold_in(key, 17), -4.0, 4.0, (JUDGES, D, KVW), jnp.float32) / math.sqrt(D)
    return matrix.astype(jnp.bfloat16)


def draw_reward_head(key, part):
    matrix = jax.random.truncated_normal(jax.random.fold_in(key, 21), -4.0, 4.0, (JUDGES, D), jnp.float32) / math.sqrt(D // 4)
    return matrix.astype(jnp.float32)


def set_ends(entries, key, smallest, largest):
    longest = entries.shape.index(max(entries.shape))
    spots = []
    for shift in (0, 1):
        where = [jax.random.randint(jax.random.fold_in(key, axis), (), 0, length) for axis, length in enumerate(entries.shape)]
        where[longest] = (where[longest] + shift) % entries.shape[longest]
        spots.append(tuple(where))
    return entries.at[spots[0]].set(smallest).at[spots[1]].set(largest)


def block_scale(key, dims, cuts, least, high):
    def one(axis_at, parts):
        steps = jax.random.uniform(jax.random.fold_in(jax.random.fold_in(key, 6), axis_at), (parts,), jnp.float32, least / len(cuts), high / len(cuts))
        return jnp.repeat(jnp.exp(steps), dims[axis_at] // parts).reshape((-1,) + (1,) * (len(dims) - axis_at - 1))

    level = one(*cuts[0])
    for cut in cuts[1:]:
        level = level * one(*cut)
    return level


def noise(rng, extent, scale, limit, cuts=(), kind=jnp.bfloat16):
    loudness = block_scale(rng, extent, cuts, -0.22, 0.18) if cuts else 1.0
    values = jax.random.normal(rng, extent, jnp.float32) * scale * loudness
    return jnp.minimum(jnp.maximum(values, -limit), limit).astype(kind)


def setup_inputs(seed: int = 0) -> dict:
    streams_of = jax.random.split(jax.random.key(seed), 15)
    hidden = draw_hidden(jax.random.fold_in(streams_of[14], 71), 0)
    lengths = set_ends(jax.random.randint(streams_of[1], (CANDS,), LEN // 4, LEN + 1), jax.random.fold_in(streams_of[1], 1), LEN // 4, LEN).astype(jnp.int32)
    duplicate_group_index = draw_duplicate_group_index(jax.random.fold_in(streams_of[14], 71), 0)
    attn_gain = jnp.clip(1.0 + 0.1 * jax.random.normal(streams_of[3], (JUDGES, D), jnp.float32), 0.5, 1.5).astype(jnp.bfloat16)
    w_query = draw_w_query(jax.random.fold_in(streams_of[14], 71), 0)
    w_key = draw_w_key(jax.random.fold_in(streams_of[14], 71), 0)
    w_value = noise(streams_of[6], (JUDGES, D, KVW), D ** -0.5, 0.09375, ((0, 4), (1, 8)))
    w_out = noise(streams_of[7], (JUDGES, D, D), D ** -0.5, 0.09375, ((0, 4), (1, 8)))
    mlp_gain = jnp.clip(1.0 + 0.1 * jax.random.normal(streams_of[8], (JUDGES, D), jnp.float32), 0.5, 1.5).astype(jnp.bfloat16)
    w_gate = noise(streams_of[9], (JUDGES, D, FF), D ** -0.5, 0.09375, ((0, 4), (2, 8)))
    w_up = noise(streams_of[10], (JUDGES, D, FF), D ** -0.5, 0.09375, ((0, 4), (2, 8)))
    w_down = noise(streams_of[11], (JUDGES, FF, D), FF ** -0.5, 0.046875, ((0, 4), (1, 8)))
    final_gain = jnp.clip(1.0 + 0.1 * jax.random.normal(streams_of[12], (JUDGES, D), jnp.float32), 0.5, 1.5).astype(jnp.bfloat16)
    reward_head = draw_reward_head(jax.random.fold_in(streams_of[14], 71), 0)
    return {"hidden": hidden, "lengths": lengths, "duplicate_group_index": duplicate_group_index, "attn_gain": attn_gain, "w_query": w_query, "w_key": w_key, "w_value": w_value, "w_out": w_out, "mlp_gain": mlp_gain, "w_gate": w_gate, "w_up": w_up, "w_down": w_down, "final_gain": final_gain, "reward_head": reward_head}


EPS = 1e-05
ROPE_BASE = 500000.0

def normalize(v, gain):
    v = v.astype(jnp.float32)
    return v * lax.rsqrt(lax.optimization_barrier(jnp.mean(v * v, axis=-1, keepdims=True)) + EPS) * gain.astype(jnp.float32)

def angles(position):
    half = HEAD_DIM // 2
    freq = jnp.exp(jnp.arange(half, dtype=jnp.float32) * (-2.0 * math.log(ROPE_BASE) / HEAD_DIM))
    turned = position[..., None] * freq
    return (jnp.cos(turned), jnp.sin(turned))

def rotate(v, cosine, sine):
    half = HEAD_DIM // 2
    first = v[..., :half]
    second = v[..., half:]
    return jnp.concatenate([first * cosine - second * sine, second * cosine + first * sine], axis=-1)

def judge_features(x, lengths, attn_gain, w_query, w_key, w_value, w_out, mlp_gain, w_gate, w_up, w_down, final_gain):
    groups = HEADS // KV_HEADS
    last_index = jnp.arange(CANDS, dtype=jnp.int32) * LEN + lengths - 1
    x_last = x[last_index].astype(jnp.float32)
    q_norm = normalize(x_last, attn_gain).astype(jnp.bfloat16)
    query = jnp.dot(q_norm, w_query, preferred_element_type=jnp.float32).reshape(CANDS, HEADS, HEAD_DIM)
    cosine, sine = angles((lengths - 1).astype(jnp.float32))
    query = rotate(query, cosine[:, None, :], sine[:, None, :]).astype(jnp.bfloat16)
    query = query.reshape(CANDS, KV_HEADS, groups, HEAD_DIM)
    key_cos, key_sin = angles(jnp.arange(LEN, dtype=jnp.float32))
    blocks = x.reshape(CANDS, LEN, D)

    def attend(item):
        block, q_one, length = item
        tok_norm = normalize(block, attn_gain).astype(jnp.bfloat16)
        keys = jnp.dot(tok_norm, w_key, preferred_element_type=jnp.float32).reshape(LEN, KV_HEADS, HEAD_DIM)
        keys = rotate(keys, key_cos[:, None, :], key_sin[:, None, :]).astype(jnp.bfloat16)
        values = jnp.dot(tok_norm, w_value, preferred_element_type=jnp.float32).astype(jnp.bfloat16)
        values = values.reshape(LEN, KV_HEADS, HEAD_DIM)
        scores = jnp.einsum('kgd,lkd->kgl', q_one.astype(jnp.float32), keys.astype(jnp.float32)) * HEAD_DIM ** (-0.5)
        valid = jnp.arange(LEN, dtype=jnp.int32) < length
        scores = jnp.where(valid, scores, -1e+30)
        top = lax.optimization_barrier(jnp.max(scores, axis=-1, keepdims=True))
        expo = jnp.exp(scores - top)
        probs = (expo / lax.optimization_barrier(jnp.sum(expo, axis=-1, keepdims=True))).astype(jnp.bfloat16)
        mixed = jnp.einsum('kgl,lkd->kgd', probs.astype(jnp.float32), values.astype(jnp.float32))
        return mixed.reshape(D).astype(jnp.bfloat16)
    mixed = lax.map(attend, (blocks, query, lengths))
    after_attn = x_last + jnp.dot(mixed, w_out, preferred_element_type=jnp.float32)
    m_norm = normalize(after_attn, mlp_gain).astype(jnp.bfloat16)
    gate = jnp.dot(m_norm, w_gate, preferred_element_type=jnp.float32)
    up = jnp.dot(m_norm, w_up, preferred_element_type=jnp.float32)
    act = (jax.nn.silu(gate) * up).astype(jnp.bfloat16)
    after_mlp = after_attn + jnp.dot(act, w_down, preferred_element_type=jnp.float32)
    return normalize(after_mlp, final_gain)

def remaining_candidates(judge_panel, duplicate_group_index, duplicate_groups):
    same = duplicate_group_index[:, None] == duplicate_group_index[None, :]
    top = lax.optimization_barrier(jnp.max(jnp.where(same, judge_panel[None, :], -1e+30), axis=1))
    expo = jnp.exp(judge_panel - top)
    total = lax.optimization_barrier(jnp.sum(jnp.where(same, expo[None, :], 0.0), axis=1))
    weight_values = expo / total
    panel_member = (duplicate_group_index[:, None] == jnp.arange(duplicate_groups, dtype=jnp.int32)[None, :]).astype(jnp.float32)
    return (weight_values, panel_member)

def reference(hidden, lengths, duplicate_group_index, attn_gain, w_query, w_key, w_value, w_out, mlp_gain, w_gate, w_up, w_down, final_gain, reward_head):
    total_features = jnp.zeros((CANDS, D), jnp.float32)
    score_total = jnp.zeros((CANDS,), jnp.float32)
    for judge in range(N_JUDGE):
        features = judge_features(hidden[judge], lengths, attn_gain[judge], w_query[judge], w_key[judge], w_value[judge], w_out[judge], mlp_gain[judge], w_gate[judge], w_up[judge], w_down[judge], final_gain[judge])
        score = jnp.dot(features, reward_head[judge], precision=lax.Precision.HIGHEST)
        total_features = total_features + features
        score_total = score_total + score
    mean_features = total_features / N_JUDGE
    judge_panel = score_total / N_JUDGE
    weight_values, panel_member = remaining_candidates(judge_panel, duplicate_group_index, DUPLICATE_GROUPS)
    cluster_features = jnp.dot(panel_member.T, weight_values[:, None] * mean_features, precision=lax.Precision.HIGHEST)
    return (weight_values, cluster_features)
```

```python
import functools
import math

import jax
import jax.numpy as jnp
from jax import lax
from jax.experimental import pallas as pl
from jax.experimental.pallas import tpu as pltpu
from jax.sharding import PartitionSpec as P

KV_HEADS = 8
HEAD_DIM = 128
LEN = 512


EPS = 1e-05
ROPE_BASE = 500000.0


def row_scale(v):
    return lax.rsqrt(jnp.mean(v * v, axis=-1, keepdims=True) + EPS)


def angles(position):
    half = HEAD_DIM // 2
    freq = jnp.exp(jnp.arange(half, dtype=jnp.float32) * (-2.0 * math.log(ROPE_BASE) / HEAD_DIM))
    turned = position[..., None] * freq
    return (jnp.cos(turned), jnp.sin(turned))


def rotate(v, cosine, sine):
    half = HEAD_DIM // 2
    first = v[..., :half]
    second = v[..., half:]
    return jnp.concatenate(
        [first * cosine - second * sine, second * cosine + first * sine], axis=-1
    )


def remaining_candidates(judge_panel, duplicate_group_index, duplicate_groups):
    same = duplicate_group_index[:, None] == duplicate_group_index[None, :]
    top = jnp.max(jnp.where(same, judge_panel[None, :], -1e30), axis=1)
    expo = jnp.exp(judge_panel - top)
    total = jnp.sum(jnp.where(same, expo[None, :], 0.0), axis=1)
    weight_values = expo / total
    panel_member = (
        duplicate_group_index[:, None] == jnp.arange(duplicate_groups, dtype=jnp.int32)[None, :]
    ).astype(jnp.float32)
    return (weight_values, panel_member)


def peer_of(me, k, n):
    return lax.rem(me + k, n)


def greet(axes):
    barrier = pltpu.get_barrier_semaphore()
    total = 0
    for axis, n in axes:
        me = lax.axis_index(axis)

        def signal(k, carry, axis=axis, n=n, me=me):
            pl.semaphore_signal(
                barrier,
                inc=1,
                device_id={axis: peer_of(me, k, n)},
                device_id_type=pl.DeviceIdType.MESH,
            )
            return carry

        lax.fori_loop(1, n, signal, 0)
        total += n - 1
    pl.semaphore_wait(barrier, total)


def remote(src, dst, send_sem, recv_sem, axis, peer):
    return pltpu.make_async_remote_copy(
        src_ref=src,
        dst_ref=dst,
        send_sem=send_sem,
        recv_sem=recv_sem,
        device_id={axis: peer},
        device_id_type=pl.DeviceIdType.MESH,
    )


def start_all(axis, n, source, dst, sems):
    me = lax.axis_index(axis)

    def one(k, carry):
        peer = peer_of(me, k, n)
        remote(source(peer), dst.at[me], sems.at[0, k], sems.at[1, k], axis, peer).start()
        return carry

    lax.fori_loop(1, n, one, 0)


def recv_all(axis, n, dst, sems):
    me = lax.axis_index(axis)

    def one(k, carry):
        sender = peer_of(me, n - k, n)
        block = dst.at[sender]
        remote(block, block, sems.at[0, k], sems.at[1, k], axis, sender).wait_recv()
        return carry

    lax.fori_loop(1, n, one, 0)


def sent_all(axis, n, dst, sems):
    me = lax.axis_index(axis)

    def one(k, carry):
        block = dst.at[me]
        remote(block, block, sems.at[0, k], sems.at[1, k], axis, peer_of(me, k, n)).wait_send()
        return carry

    lax.fori_loop(1, n, one, 0)


def attend_kernel(
    n,
    seq_dev,
    own_len,
    tokens,
    w_query,
    w_key,
    w_value,
    last_pack,
    gain_pack,
    q_cos,
    q_sin,
    k_cos,
    k_sin,
    mixed_out,
    last_out,
    gain_out,
    wk,
    tn,
    acc,
    wq,
    wv,
    tok,
    lp,
    gp,
    xl,
    gain,
    qp,
    qr,
    qs,
    pr,
    pt,
    ptr,
    part,
    got,
    ring_send,
    ring_recv,
    local_sem,
    tok_sem,
    last_sem,
    gain_sem,
    q_sem,
    pt_sem,
    got_sem,
):
    axis = "fsdp"
    me = lax.axis_index(axis)
    rows = w_key.shape[0]
    half_cols = wk.shape[-1]
    sub = rows // 2
    width = tokens.shape[1]
    tok_dev = tokens.shape[0]
    cands = xl.shape[0]
    half_n = n // 2
    odd = lax.rem(me, 2)
    pos = (1 - odd) * (me // 2) + odd * (n - 1 - me // 2)

    def at_pos(p):
        p = lax.rem(p, n)
        back = p // half_n
        return (1 - back) * (2 * p) + back * (2 * (n - 1 - p) + 1)

    after = at_pos(pos + 1)
    before = at_pos(pos + n - 1)

    def copies(step, direction, j):
        if direction == 0:
            owner, target = at_pos(pos + n - step), after
        else:
            owner, target = at_pos(pos + step), before
        piece = wk.at[owner, direction, pl.ds(j * sub, sub), :]
        sems = (ring_send.at[direction, j, step], ring_recv.at[direction, j, step])
        return piece, target, sems

    own_key = [
        pltpu.make_async_copy(
            w_key.at[:, pl.ds(d * half_cols, half_cols)], wk.at[me, d], local_sem.at[d]
        )
        for d in range(2)
    ]
    for copy in own_key:
        copy.start()
    query_copy = pltpu.make_async_copy(w_query, wq, local_sem.at[2])
    value_copy = pltpu.make_async_copy(w_value, wv, local_sem.at[3])
    chunk = tok.shape[1]
    chunks = tok_dev // chunk

    def tok_copy(c):
        return pltpu.make_async_copy(
            tokens.at[pl.ds(c * chunk, chunk), :], tok.at[lax.rem(c, 2)], tok_sem.at[lax.rem(c, 2)]
        )

    tok_copy(0).start()
    greet([(axis, n)])
    start_all(axis, n, lambda peer: last_pack, lp, last_sem)
    start_all(axis, n, lambda peer: gain_pack, gp, gain_sem)
    for copy in own_key:
        copy.wait()
    for j in range(2):
        for d in range(2):
            piece, target, sems = copies(0, d, j)
            remote(piece, piece, *sems, axis, target).start()
    query_copy.start()
    value_copy.start()
    lp[me] = last_pack[...]
    gp[me] = gain_pack[...]
    recv_all(axis, n, gp, gain_sem)
    for o in range(n):
        gain[0:1, o * rows : (o + 1) * rows] = gp[o, 0:1, :]

    def normalise(c, carry):
        @pl.when(c < chunks - 1)
        def _():
            tok_copy(c + 1).start()

        tok_copy(c).wait()
        v = tok[lax.rem(c, 2)].astype(jnp.float32)
        v = (v * row_scale(v) * gain[...]).astype(jnp.bfloat16)
        for o in range(n):
            tn[o, pl.ds(pl.multiple_of(c * chunk, chunk), chunk), :] = v[:, o * rows : (o + 1) * rows]
        return carry

    lax.fori_loop(0, chunks, normalise, 0)
    tile = 256

    def multiply(owner, d, first):
        def one(i, carry):
            r = pl.ds(pl.multiple_of(i * tile, tile), tile)
            term = jnp.dot(tn[owner, r, :], wk[owner, d], preferred_element_type=jnp.float32)
            if first:
                acc[d, r, :] = term
            else:
                acc[d, r, :] += term
            return carry

        lax.fori_loop(0, tok_dev // tile, one, 0)

    def take(step):
        for j in range(2):
            for d in range(2):
                piece, target, sems = copies(step, d, j)
                owner = at_pos(pos + n - 1 - step) if d == 0 else at_pos(pos + 1 + step)
                arrived = wk.at[owner, d, pl.ds(j * sub, sub), :]
                remote(arrived, arrived, *sems, axis, target).wait_recv()

                @pl.when(step < n - 2)
                def _():
                    piece, target, sems = copies(step + 1, d, j)
                    remote(piece, piece, *sems, axis, target).start()

    take(0)
    for d in range(2):
        multiply(me, d, True)
    recv_all(axis, n, lp, last_sem)
    pack_width = lp.shape[2]
    blocks = width // pack_width
    for o in range(n):
        for b in range(blocks):
            xl[o * seq_dev : (o + 1) * seq_dev, b * pack_width : (b + 1) * pack_width] = lp[
                o, b * seq_dev : (b + 1) * seq_dev, :
            ]
    last_out[...] = xl[...]
    gain_out[...] = gp[...]
    query_copy.wait()
    v = xl[...]
    q = jnp.dot(
        (v * row_scale(v) * gain[...]).astype(jnp.bfloat16),
        wq[...],
        preferred_element_type=jnp.float32,
    )
    heads_dev = q.shape[1] // HEAD_DIM
    qp[...] = jnp.zeros_like(qp)
    for h in range(heads_dev):
        one = q[:, h * HEAD_DIM : (h + 1) * HEAD_DIM]
        one = one * q_cos[...] + pltpu.roll(one, HEAD_DIM // 2, 1) * q_sin[...]
        one = one.astype(jnp.bfloat16).astype(jnp.float32)
        for o in range(n):
            qp[o, h * seq_dev : (h + 1) * seq_dev, :] = one[o * seq_dev : (o + 1) * seq_dev, :]
    start_all(axis, n, lambda peer: qp.at[peer], qr, q_sem)
    qr[me] = qp[me]

    def use(step):
        multiply(at_pos(pos + n - 1 - step), 0, False)
        multiply(at_pos(pos + 1 + step), 1, False)

    use(0)

    def ring(step, carry):
        take(step)
        use(step)
        return carry

    lax.fori_loop(1, n - 1, ring, 0)
    recv_all(axis, n, qr, q_sem)
    groups = width // HEAD_DIM // KV_HEADS
    qs[...] = jnp.zeros_like(qs)
    for head in range(KV_HEADS * groups):
        for s in range(seq_dev):
            row = (head % heads_dev) * seq_dev + s
            qs[s, head // groups, head % groups : head % groups + 1, :] = qr[
                head // heads_dev, row : row + 1, :
            ]
    per_half = half_cols // HEAD_DIM
    for s in range(seq_dev):
        valid = lax.broadcasted_iota(jnp.int32, (8, LEN), 1) < own_len[s]
        for k in range(KV_HEADS):
            key = acc[
                k // per_half,
                s * LEN : (s + 1) * LEN,
                k % per_half * HEAD_DIM : (k % per_half + 1) * HEAD_DIM,
            ]
            key = (key * k_cos[...] + pltpu.roll(key, HEAD_DIM // 2, 1) * k_sin[...]).astype(
                jnp.bfloat16
            )
            scores = lax.dot_general(
                qs[s, k].astype(jnp.bfloat16),
                key,
                (((1,), (1,)), ((), ())),
                preferred_element_type=jnp.float32,
            ) * HEAD_DIM ** (-0.5)
            scores = jnp.where(valid, scores, -1e30)
            expo = jnp.exp(scores - jnp.max(scores, axis=-1, keepdims=True))
            pr[s, k] = expo / jnp.sum(expo, axis=-1, keepdims=True)
    each = KV_HEADS * 8
    for s in range(seq_dev):
        probs = pr[s].reshape(each, LEN).astype(jnp.bfloat16)

        def spread(o, carry, s=s, probs=probs):
            one = jnp.dot(
                probs, tn[o, s * LEN : (s + 1) * LEN, :], preferred_element_type=jnp.float32
            ).astype(jnp.bfloat16)
            pt[o, s * each : (s + 1) * each, :] = one
            return carry

        lax.fori_loop(0, n, spread, 0)
    start_all(axis, n, lambda peer: pt.at[peer], ptr, pt_sem)
    ptr[me] = pt[me]
    value_copy.wait()
    recv_all(axis, n, ptr, pt_sem)
    kpd = max(1, KV_HEADS // n)

    def project(src, carry):
        full = jnp.dot(ptr[src], wv[...], preferred_element_type=jnp.float32)
        for o in range(n):
            for i in range(kpd):
                k = o * heads_dev // groups + i
                for s in range(seq_dev):
                    part[o, i * seq_dev + s, src] = full[
                        s * each + k * 8 : s * each + (k + 1) * 8, k * HEAD_DIM : (k + 1) * HEAD_DIM
                    ]
        return carry

    lax.fori_loop(0, n, project, 0)
    start_all(axis, n, lambda peer: part.at[peer], got, got_sem)
    got[me] = part[me]
    recv_all(axis, n, got, got_sem)
    total = got[0]
    for o in range(1, n):
        total = total + got[o]
    mixed_out[...] = total

    def drain(step, carry):
        for j in range(2):
            for d in range(2):
                piece, target, sems = copies(step, d, j)
                remote(piece, piece, *sems, axis, target).wait_send()
        return carry

    lax.fori_loop(0, n - 1, drain, 0)
    sent_all(axis, n, lp, last_sem)
    sent_all(axis, n, gp, gain_sem)
    sent_all(axis, n, qr, q_sem)
    sent_all(axis, n, ptr, pt_sem)
    sent_all(axis, n, got, got_sem)


def feed_kernel(
    n,
    judges,
    mixed,
    last_cols,
    gains,
    gain_final,
    reward,
    w_out,
    w_gate,
    w_up,
    w_down,
    feat_out,
    score_out,
    wo,
    wg,
    wu,
    wd,
    send_a,
    recv_a,
    full,
    m_norm,
    send_d,
    recv_d,
    stats,
    feats,
    scores,
    local_sem,
    gate_sem,
    up_sem,
    a_sem,
    g_sem,
    d_sem,
    s_sem,
    f_sem,
    c_sem,
):
    axis = "fsdp"
    me = lax.axis_index(axis)
    judge = lax.axis_index("judge")
    rows = w_out.shape[0]
    width = w_out.shape[1]
    cands = mixed.shape[0]
    hidden = w_gate.shape[1]
    out_copy = pltpu.make_async_copy(w_out, wo, local_sem.at[0])
    down_copy = pltpu.make_async_copy(w_down, wd, local_sem.at[1])
    out_copy.start()

    def columns(o):
        return pl.ds(pl.multiple_of(o * rows, rows), rows)

    def part_copies(o):
        return (
            pltpu.make_async_copy(w_gate.at[columns(o), :], wg.at[columns(o), :], gate_sem.at[o]),
            pltpu.make_async_copy(w_up.at[columns(o), :], wu.at[columns(o), :], up_sem.at[o]),
        )

    def fetch(o, carry):
        for copy in part_copies(o):
            copy.start()
        return carry

    lax.fori_loop(0, n, fetch, 0)
    down_copy.start()
    greet([(axis, n), ("judge", judges)])
    out_copy.wait()

    def attn_part(o, carry):
        send_a[o] = jnp.dot(mixed[...], wo[:, columns(o)], preferred_element_type=jnp.float32)
        return carry

    lax.fori_loop(0, n, attn_part, 0)
    start_all(axis, n, lambda peer: send_a.at[peer], recv_a, a_sem)
    recv_a[me] = send_a[me]
    recv_all(axis, n, recv_a, a_sem)
    own = recv_a[0]
    for o in range(1, n):
        own = own + recv_a[o]
    own = last_cols[...] + own
    full[me] = own
    start_all(axis, n, lambda peer: full.at[me], full, g_sem)
    recv_all(axis, n, full, g_sem)
    square = full[0] * full[0]
    for o in range(1, n):
        square = square + full[o] * full[o]
    scale = lax.rsqrt(jnp.sum(square, axis=-1, keepdims=True) / width + EPS)
    for o in range(n):
        m_norm[o] = (full[o] * scale * gains[o, 1:2, :]).astype(jnp.bfloat16)

    def widen(o, carry):
        for copy in part_copies(o):
            copy.wait()
        one = m_norm[o]
        gate = jnp.dot(one, wg[columns(o), :], preferred_element_type=jnp.float32)
        up = jnp.dot(one, wu[columns(o), :], preferred_element_type=jnp.float32)
        return (carry[0] + gate, carry[1] + up)

    zero = jnp.zeros((cands, hidden), jnp.float32)
    gate, up = lax.fori_loop(0, n, widen, (zero, zero))
    act = (gate / (1.0 + jnp.exp(-gate)) * up).astype(jnp.bfloat16)
    down_copy.wait()

    def down_part(k, carry):
        o = peer_of(me, k, n)
        send_d[o] = jnp.dot(act, wd[:, columns(o)], preferred_element_type=jnp.float32)

        remote(send_d.at[o], recv_d.at[me], d_sem.at[0, k], d_sem.at[1, k], axis, o).start()
        return carry

    lax.fori_loop(1, n, down_part, 0)
    recv_d[me] = jnp.dot(act, wd[:, columns(me)], preferred_element_type=jnp.float32)
    recv_all(axis, n, recv_d, d_sem)
    mlp = recv_d[0]
    for o in range(1, n):
        mlp = mlp + recv_d[o]
    mlp = full[me] + mlp
    feat = mlp * gain_final[...]
    lane = lax.broadcasted_iota(jnp.int32, (cands, HEAD_DIM), 1)
    stats[me] = jnp.where(
        lane == 0,
        jnp.sum(mlp * mlp, axis=-1, keepdims=True),
        jnp.sum(feat * reward[...], axis=-1, keepdims=True),
    )
    start_all(axis, n, lambda peer: stats.at[me], stats, s_sem)
    recv_all(axis, n, stats, s_sem)
    total = stats[0]
    for o in range(1, n):
        total = total + stats[o]
    scale = lax.rsqrt(total[:, 0:1] / width + EPS)
    feats[judge] = feat * scale
    scores[judge] = total * scale
    start_all("judge", judges, lambda peer: feats.at[judge], feats, f_sem)
    start_all("judge", judges, lambda peer: scores.at[judge], scores, c_sem)
    recv_all("judge", judges, feats, f_sem)
    recv_all("judge", judges, scores, c_sem)
    feat = feats[0]
    score = scores[0]
    for j in range(1, judges):
        feat = feat + feats[j]
        score = score + scores[j]
    feat_out[...] = feat
    score_out[...] = score
    sent_all(axis, n, recv_a, a_sem)
    sent_all(axis, n, full, g_sem)
    sent_all(axis, n, recv_d, d_sem)
    sent_all(axis, n, stats, s_sem)
    sent_all("judge", judges, feats, f_sem)
    sent_all("judge", judges, scores, c_sem)


def body(
    hidden,
    lengths,
    duplicate_group_index,
    attn_gain,
    w_query,
    w_key,
    w_value,
    w_out,
    mlp_gain,
    w_gate,
    w_up,
    w_down,
    final_gain,
    reward_head,
):
    judges = lax.axis_size("judge")
    n = lax.axis_size("fsdp")
    me = lax.axis_index("fsdp")
    tokens = hidden[0]
    tok_dev, width = tokens.shape
    seq_dev = tok_dev // LEN
    cands = lengths.shape[0]
    duplicate_groups = cands // 4
    heads = width // HEAD_DIM
    groups = heads // KV_HEADS
    cols = width // n
    heads_dev = cols // HEAD_DIM
    kvw = w_key.shape[2]
    f32, bf16 = jnp.float32, jnp.bfloat16
    own_len = lax.dynamic_slice_in_dim(lengths, me * seq_dev, seq_dev)
    own_last = jnp.concatenate(
        [
            lax.dynamic_slice_in_dim(tokens, s * LEN + own_len[s] - 1, 1, 0)
            for s in range(seq_dev)
        ],
        axis=0,
    ).astype(f32)
    pack_width = seq_dev * width // 8
    last_pack = own_last.reshape(seq_dev, width // pack_width, pack_width)
    last_pack = last_pack.transpose(1, 0, 2).reshape(8, pack_width)
    gain_pack = jnp.concatenate(
        [attn_gain, mlp_gain, final_gain, jnp.zeros((5, cols), bf16)], axis=0
    ).astype(f32)

    def table(position):
        cosine, sine = angles(position)
        return (
            jnp.concatenate([cosine, cosine], axis=-1),
            jnp.concatenate([-sine, sine], axis=-1),
        )

    q_cos, q_sin = table((lengths - 1).astype(f32))
    k_cos, k_sin = table(jnp.arange(LEN, dtype=f32))
    kpd = max(1, KV_HEADS // n)
    q_rows = max(8, heads_dev * seq_dev)
    each = KV_HEADS * 8
    vmem = pl.BlockSpec(memory_space=pltpu.VMEM)
    anywhere = pl.BlockSpec(memory_space=pl.ANY)
    dma = pltpu.SemaphoreType.DMA
    mixed_pack, x_last, gains = pl.pallas_call(
        functools.partial(attend_kernel, n, seq_dev),
        out_shape=(
            jax.ShapeDtypeStruct((kpd * seq_dev, n, 8, HEAD_DIM), f32),
            jax.ShapeDtypeStruct((cands, width), f32),
            jax.ShapeDtypeStruct((n, 8, cols), f32),
        ),
        in_specs=[pl.BlockSpec(memory_space=pltpu.SMEM)] + [anywhere] * 4 + [vmem] * 6,
        out_specs=(vmem, vmem, vmem),
        scratch_shapes=[
            pltpu.VMEM((n, 2, cols, kvw // 2), bf16),
            pltpu.VMEM((n, tok_dev, cols), bf16),
            pltpu.VMEM((2, tok_dev, kvw // 2), f32),
            pltpu.VMEM((width, cols), bf16),
            pltpu.VMEM((cols, kvw), bf16),
            pltpu.VMEM((2, 128, width), bf16),
            pltpu.VMEM((n, 8, pack_width), f32),
            pltpu.VMEM((n, 8, cols), f32),
            pltpu.VMEM((cands, width), f32),
            pltpu.VMEM((1, width), f32),
            pltpu.VMEM((n, q_rows, HEAD_DIM), f32),
            pltpu.VMEM((n, q_rows, HEAD_DIM), f32),
            pltpu.VMEM((seq_dev, KV_HEADS, 8, HEAD_DIM), f32),
            pltpu.VMEM((seq_dev, KV_HEADS, 8, LEN), f32),
            pltpu.VMEM((n, seq_dev * each, cols), bf16),
            pltpu.VMEM((n, seq_dev * each, cols), bf16),
            pltpu.VMEM((n, kpd * seq_dev, n, 8, HEAD_DIM), f32),
            pltpu.VMEM((n, kpd * seq_dev, n, 8, HEAD_DIM), f32),
            dma((2, 2, n)),
            dma((2, 2, n)),
            dma((4,)),
            dma((2,)),
            dma((2, n)),
            dma((2, n)),
            dma((2, n)),
            dma((2, n)),
            dma((2, n)),
        ],
        compiler_params=pltpu.CompilerParams(
            collective_id=0, has_side_effects=True, vmem_limit_bytes=50 * 2**20
        ),
    )(
        own_len,
        tokens,
        w_query[0],
        w_key[0],
        w_value[0],
        last_pack,
        gain_pack,
        q_cos,
        q_sin,
        k_cos,
        k_sin,
    )
    mixed = mixed_pack.reshape(kpd, seq_dev, n, 8, HEAD_DIM)[:, :, :, :groups]
    mixed = mixed.transpose(2, 1, 0, 3, 4).reshape(cands, kpd * groups * HEAD_DIM).astype(bf16)
    first = lax.rem(me * heads_dev, groups) if heads_dev < groups else 0
    mixed = lax.dynamic_slice_in_dim(mixed, first * HEAD_DIM, cols, 1)
    last_cols = lax.dynamic_slice_in_dim(x_last, me * cols, cols, 1)
    reward = lax.dynamic_slice_in_dim(reward_head, me * cols, cols, 1)
    hidden_dev = w_gate.shape[2]
    total_cols, score_total = pl.pallas_call(
        functools.partial(feed_kernel, n, judges),
        out_shape=(
            jax.ShapeDtypeStruct((cands, cols), f32),
            jax.ShapeDtypeStruct((cands, HEAD_DIM), f32),
        ),
        in_specs=[vmem] * 5 + [anywhere] * 4,
        out_specs=(vmem, vmem),
        scratch_shapes=[
            pltpu.VMEM((cols, width), bf16),
            pltpu.VMEM((width, hidden_dev), bf16),
            pltpu.VMEM((width, hidden_dev), bf16),
            pltpu.VMEM((hidden_dev, width), bf16),
            pltpu.VMEM((n, cands, cols), f32),
            pltpu.VMEM((n, cands, cols), f32),
            pltpu.VMEM((n, cands, cols), f32),
            pltpu.VMEM((n, cands, cols), bf16),
            pltpu.VMEM((n, cands, cols), f32),
            pltpu.VMEM((n, cands, cols), f32),
            pltpu.VMEM((n, cands, HEAD_DIM), f32),
            pltpu.VMEM((judges, cands, cols), f32),
            pltpu.VMEM((judges, cands, HEAD_DIM), f32),
            dma((2,)),
            dma((n,)),
            dma((n,)),
            dma((2, n)),
            dma((2, n)),
            dma((2, n)),
            dma((2, n)),
            dma((2, judges)),
            dma((2, judges)),
        ],
        compiler_params=pltpu.CompilerParams(
            collective_id=1, has_side_effects=True, vmem_limit_bytes=60 * 2**20
        ),
    )(
        mixed,
        last_cols,
        gains,
        final_gain.astype(f32),
        reward,
        w_out[0],
        w_gate[0],
        w_up[0],
        w_down[0],
    )
    weight_values, panel_member = remaining_candidates(
        score_total[:, 1] / judges, duplicate_group_index, duplicate_groups
    )
    cluster_cols = jnp.dot(
        panel_member.T,
        weight_values[:, None] * (total_cols / judges),
        precision=lax.Precision.HIGHEST,
    )
    return (weight_values, cluster_cols)


def solution(mesh):
    in_specs = (
        P("judge", "fsdp", None),
        P(),
        P(),
        P("judge", "fsdp"),
        P("judge", None, "fsdp"),
        P("judge", "fsdp", None),
        P("judge", "fsdp", None),
        P("judge", "fsdp", None),
        P("judge", "fsdp"),
        P("judge", None, "fsdp"),
        P("judge", None, "fsdp"),
        P("judge", "fsdp", None),
        P("judge", "fsdp"),
        P("judge", None),
    )
    out_specs = (P(), P(None, "fsdp"))
    return jax.shard_map(body, mesh=mesh, in_specs=in_specs, out_specs=out_specs, check_vma=False)
```

```python
import functools
import math

import jax
import jax.numpy as jnp
from jax import lax
from jax.experimental import pallas as pl
from jax.experimental.pallas import tpu as pltpu
from jax.sharding import PartitionSpec as P

KV_HEADS = 8
HEAD_DIM = 128
LEN = 512


EPS = 1e-05
ROPE_BASE = 500000.0


def row_scale(v):
    return lax.rsqrt(jnp.mean(v * v, axis=-1, keepdims=True) + EPS)


def angles(position):
    half = HEAD_DIM // 2
    freq = jnp.exp(jnp.arange(half, dtype=jnp.float32) * (-2.0 * math.log(ROPE_BASE) / HEAD_DIM))
    turned = position[..., None] * freq
    return (jnp.cos(turned), jnp.sin(turned))


def rotate(v, cosine, sine):
    half = HEAD_DIM // 2
    first = v[..., :half]
    second = v[..., half:]
    return jnp.concatenate(
        [first * cosine - second * sine, second * cosine + first * sine], axis=-1
    )


def remaining_candidates(judge_panel, duplicate_group_index, duplicate_groups):
    same = duplicate_group_index[:, None] == duplicate_group_index[None, :]
    top = jnp.max(jnp.where(same, judge_panel[None, :], -1e30), axis=1)
    expo = jnp.exp(judge_panel - top)
    total = jnp.sum(jnp.where(same, expo[None, :], 0.0), axis=1)
    weight_values = expo / total
    panel_member = (
        duplicate_group_index[:, None] == jnp.arange(duplicate_groups, dtype=jnp.int32)[None, :]
    ).astype(jnp.float32)
    return (weight_values, panel_member)


def peer_of(me, k, n):
    return lax.rem(me + k, n)


def greet(axes):
    barrier = pltpu.get_barrier_semaphore()
    total = 0
    for axis, n in axes:
        me = lax.axis_index(axis)

        def signal(k, carry, axis=axis, n=n, me=me):
            pl.semaphore_signal(
                barrier,
                inc=1,
                device_id={axis: peer_of(me, k, n)},
                device_id_type=pl.DeviceIdType.MESH,
            )
            return carry

        lax.fori_loop(1, n, signal, 0)
        total += n - 1
    pl.semaphore_wait(barrier, total)


def remote(src, dst, send_sem, recv_sem, axis, peer):
    return pltpu.make_async_remote_copy(
        src_ref=src,
        dst_ref=dst,
        send_sem=send_sem,
        recv_sem=recv_sem,
        device_id={axis: peer},
        device_id_type=pl.DeviceIdType.MESH,
    )


def start_all(axis, n, source, dst, sems):
    me = lax.axis_index(axis)

    def one(k, carry):
        peer = peer_of(me, k, n)
        remote(source(peer), dst.at[me], sems.at[0, k], sems.at[1, k], axis, peer).start()
        return carry

    lax.fori_loop(1, n, one, 0)


def recv_all(axis, n, dst, sems):
    me = lax.axis_index(axis)

    def one(k, carry):
        sender = peer_of(me, n - k, n)
        block = dst.at[sender]
        remote(block, block, sems.at[0, k], sems.at[1, k], axis, sender).wait_recv()
        return carry

    lax.fori_loop(1, n, one, 0)


def sent_all(axis, n, dst, sems):
    me = lax.axis_index(axis)

    def one(k, carry):
        block = dst.at[me]
        remote(block, block, sems.at[0, k], sems.at[1, k], axis, peer_of(me, k, n)).wait_send()
        return carry

    lax.fori_loop(1, n, one, 0)


def attend_kernel(
    n,
    seq_dev,
    own_len,
    tokens,
    w_query,
    w_key,
    w_value,
    last_pack,
    gain_pack,
    q_cos,
    q_sin,
    k_cos,
    k_sin,
    mixed_out,
    last_out,
    gain_out,
    wk,
    tn,
    acc,
    wq,
    wv,
    tok,
    lp,
    gp,
    xl,
    gain,
    qp,
    qr,
    qs,
    pr,
    pt,
    ptr,
    proj,
    part,
    got,
    ring_send,
    ring_recv,
    local_sem,
    tok_sem,
    last_sem,
    gain_sem,
    q_sem,
    pt_sem,
    got_sem,
):
    axis = "fsdp"
    me = lax.axis_index(axis)
    rows = w_key.shape[0]
    half_cols = wk.shape[-1]
    sub = rows // 2
    width = tokens.shape[1]
    tok_dev = tokens.shape[0]
    cands = xl.shape[0]
    half_n = n // 2
    odd = lax.rem(me, 2)
    pos = (1 - odd) * (me // 2) + odd * (n - 1 - me // 2)

    def at_pos(p):
        p = lax.rem(p, n)
        back = p // half_n
        return (1 - back) * (2 * p) + back * (2 * (n - 1 - p) + 1)

    after = at_pos(pos + 1)
    before = at_pos(pos + n - 1)

    def copies(step, direction, j):
        if direction == 0:
            owner, target = at_pos(pos + n - step), after
        else:
            owner, target = at_pos(pos + step), before
        piece = wk.at[owner, direction, pl.ds(j * sub, sub), :]
        sems = (ring_send.at[direction, j, step], ring_recv.at[direction, j, step])
        return piece, target, sems

    own_key = [
        pltpu.make_async_copy(
            w_key.at[:, pl.ds(d * half_cols, half_cols)], wk.at[me, d], local_sem.at[d]
        )
        for d in range(2)
    ]
    for copy in own_key:
        copy.start()
    query_copy = pltpu.make_async_copy(w_query, wq, local_sem.at[2])
    value_copy = pltpu.make_async_copy(w_value, wv, local_sem.at[3])
    chunk = tok.shape[1]
    chunks = tok_dev // chunk

    def tok_copy(c):
        return pltpu.make_async_copy(
            tokens.at[pl.ds(c * chunk, chunk), :], tok.at[lax.rem(c, 2)], tok_sem.at[lax.rem(c, 2)]
        )

    tok_copy(0).start()
    greet([(axis, n)])
    start_all(axis, n, lambda peer: last_pack, lp, last_sem)
    start_all(axis, n, lambda peer: gain_pack, gp, gain_sem)
    for copy in own_key:
        copy.wait()
    for j in range(2):
        for d in range(2):
            piece, target, sems = copies(0, d, j)
            remote(piece, piece, *sems, axis, target).start()
    query_copy.start()
    value_copy.start()
    lp[me] = last_pack[...]
    gp[me] = gain_pack[...]
    recv_all(axis, n, gp, gain_sem)
    for o in range(n):
        gain[0:1, o * rows : (o + 1) * rows] = gp[o, 0:1, :]

    def normalise(c, carry):
        @pl.when(c < chunks - 1)
        def _():
            tok_copy(c + 1).start()

        tok_copy(c).wait()
        v = tok[lax.rem(c, 2)].astype(jnp.float32)
        v = (v * row_scale(v) * gain[...]).astype(jnp.bfloat16)
        for o in range(n):
            tn[o, pl.ds(pl.multiple_of(c * chunk, chunk), chunk), :] = v[:, o * rows : (o + 1) * rows]
        return carry

    tile = 256

    def multiply(owner, d, first):
        def one(i, carry):
            r = pl.ds(pl.multiple_of(i * tile, tile), tile)
            term = jnp.dot(tn[owner, r, :], wk[owner, d], preferred_element_type=jnp.float32)
            if first:
                acc[d, r, :] = term
            else:
                acc[d, r, :] += term
            return carry

        lax.fori_loop(0, tok_dev // tile, one, 0)

    def take(step):
        for j in range(2):
            for d in range(2):
                piece, target, sems = copies(step, d, j)
                owner = at_pos(pos + n - 1 - step) if d == 0 else at_pos(pos + 1 + step)
                arrived = wk.at[owner, d, pl.ds(j * sub, sub), :]
                remote(arrived, arrived, *sems, axis, target).wait_recv()

                @pl.when(step < n - 2)
                def _():
                    piece, target, sems = copies(step + 1, d, j)
                    remote(piece, piece, *sems, axis, target).start()

    def use(step):
        multiply(at_pos(pos + n - 1 - step), 0, False)
        multiply(at_pos(pos + 1 + step), 1, False)

    take(0)
    lax.fori_loop(0, chunks, normalise, 0)
    take(1)
    for d in range(2):
        multiply(me, d, True)
    use(0)
    use(1)
    take(2)
    recv_all(axis, n, lp, last_sem)
    pack_width = lp.shape[2]
    blocks = width // pack_width
    for o in range(n):
        for b in range(blocks):
            xl[o * seq_dev : (o + 1) * seq_dev, b * pack_width : (b + 1) * pack_width] = lp[
                o, b * seq_dev : (b + 1) * seq_dev, :
            ]
    last_out[...] = xl[...]
    gain_out[...] = gp[...]
    query_copy.wait()
    v = xl[...]
    q = jnp.dot(
        (v * row_scale(v) * gain[...]).astype(jnp.bfloat16),
        wq[...],
        preferred_element_type=jnp.float32,
    )
    heads_dev = q.shape[1] // HEAD_DIM
    qp[...] = jnp.zeros_like(qp)
    for h in range(heads_dev):
        one = q[:, h * HEAD_DIM : (h + 1) * HEAD_DIM]
        one = one * q_cos[...] + pltpu.roll(one, HEAD_DIM // 2, 1) * q_sin[...]
        one = one.astype(jnp.bfloat16).astype(jnp.float32)
        for o in range(n):
            qp[o, h * seq_dev : (h + 1) * seq_dev, :] = one[o * seq_dev : (o + 1) * seq_dev, :]
    start_all(axis, n, lambda peer: qp.at[peer], qr, q_sem)
    qr[me] = qp[me]
    use(2)

    def ring(step, carry):
        take(step)
        use(step)
        return carry

    lax.fori_loop(3, n - 1, ring, 0)
    recv_all(axis, n, qr, q_sem)
    groups = width // HEAD_DIM // KV_HEADS
    for head in range(KV_HEADS * groups):
        for s in range(seq_dev):
            row = (head % heads_dev) * seq_dev + s
            slot = s * groups + head % groups
            qs[head // groups, slot : slot + 1, :] = qr[head // heads_dev, row : row + 1, :]
    per_half = half_cols // HEAD_DIM
    for s in range(seq_dev):
        valid = lax.broadcasted_iota(jnp.int32, (seq_dev * groups, LEN), 1) < own_len[s]
        for k in range(KV_HEADS):
            key = acc[
                k // per_half,
                s * LEN : (s + 1) * LEN,
                k % per_half * HEAD_DIM : (k % per_half + 1) * HEAD_DIM,
            ]
            key = (key * k_cos[...] + pltpu.roll(key, HEAD_DIM // 2, 1) * k_sin[...]).astype(
                jnp.bfloat16
            )
            scores = lax.dot_general(
                qs[k].astype(jnp.bfloat16),
                key,
                (((1,), (1,)), ((), ())),
                preferred_element_type=jnp.float32,
            ) * HEAD_DIM ** (-0.5)
            scores = jnp.where(valid, scores, -1e30)
            expo = jnp.exp(scores - jnp.max(scores, axis=-1, keepdims=True))
            probs = expo / jnp.sum(expo, axis=-1, keepdims=True)
            pr[s, k * groups : (k + 1) * groups, :] = probs[s * groups : (s + 1) * groups, :]
    each = KV_HEADS * groups
    probs = [pr[s].astype(jnp.bfloat16) for s in range(seq_dev)]

    def spread(k, carry):
        o = peer_of(me, k, n)
        for s in range(seq_dev):
            pt[o, s * each : (s + 1) * each, :] = jnp.dot(
                probs[s], tn[o, s * LEN : (s + 1) * LEN, :], preferred_element_type=jnp.float32
            ).astype(jnp.bfloat16)
        remote(pt.at[o], ptr.at[me], pt_sem.at[0, k], pt_sem.at[1, k], axis, o).start()
        return carry

    lax.fori_loop(1, n, spread, 0)
    for s in range(seq_dev):
        ptr[me, s * each : (s + 1) * each, :] = jnp.dot(
            probs[s], tn[me, s * LEN : (s + 1) * LEN, :], preferred_element_type=jnp.float32
        ).astype(jnp.bfloat16)
    value_copy.wait()
    recv_all(axis, n, ptr, pt_sem)
    kpd = max(1, KV_HEADS // n)
    spread_rows = seq_dev * each
    proj[...] = jnp.dot(
        ptr[...].reshape(n * spread_rows, rows), wv[...], preferred_element_type=jnp.float32
    ).reshape(n, spread_rows, wv.shape[1])

    def project(src, carry):
        for o in range(n):
            for i in range(kpd):
                k = o * heads_dev // groups + i
                for s in range(seq_dev):
                    part[o, i, src, s * groups : (s + 1) * groups, :] = proj[
                        src,
                        s * each + k * groups : s * each + (k + 1) * groups,
                        k * HEAD_DIM : (k + 1) * HEAD_DIM,
                    ]
        return carry

    lax.fori_loop(0, n, project, 0)
    start_all(axis, n, lambda peer: part.at[peer], got, got_sem)
    got[me] = part[me]
    recv_all(axis, n, got, got_sem)
    total = got[0]
    for o in range(1, n):
        total = total + got[o]
    mixed_out[...] = total

    def drain(step, carry):
        for j in range(2):
            for d in range(2):
                piece, target, sems = copies(step, d, j)
                remote(piece, piece, *sems, axis, target).wait_send()
        return carry

    lax.fori_loop(0, n - 1, drain, 0)
    sent_all(axis, n, lp, last_sem)
    sent_all(axis, n, gp, gain_sem)
    sent_all(axis, n, qr, q_sem)
    sent_all(axis, n, ptr, pt_sem)
    sent_all(axis, n, got, got_sem)


def feed_kernel(
    n,
    judges,
    mixed,
    last_cols,
    gains,
    gain_final,
    reward,
    w_out,
    w_gate,
    w_up,
    w_down,
    feat_out,
    score_out,
    wo,
    wg,
    wu,
    wd,
    send_a,
    recv_a,
    full,
    m_norm,
    send_d,
    recv_d,
    stats,
    feats,
    scores,
    local_sem,
    gate_sem,
    up_sem,
    a_sem,
    g_sem,
    d_sem,
    s_sem,
    f_sem,
    c_sem,
):
    axis = "fsdp"
    me = lax.axis_index(axis)
    judge = lax.axis_index("judge")
    rows = w_out.shape[0]
    width = w_out.shape[1]
    cands = mixed.shape[0]
    hidden = w_gate.shape[1]
    out_copy = pltpu.make_async_copy(w_out, wo, local_sem.at[0])
    down_copy = pltpu.make_async_copy(w_down, wd, local_sem.at[1])
    out_copy.start()

    def columns(o):
        return pl.ds(pl.multiple_of(o * rows, rows), rows)

    def part_copies(o):
        return (
            pltpu.make_async_copy(w_gate.at[columns(o), :], wg.at[columns(o), :], gate_sem.at[o]),
            pltpu.make_async_copy(w_up.at[columns(o), :], wu.at[columns(o), :], up_sem.at[o]),
        )

    def fetch(o, carry):
        for copy in part_copies(o):
            copy.start()
        return carry

    lax.fori_loop(0, n, fetch, 0)
    down_copy.start()
    greet([(axis, n), ("judge", judges)])
    out_copy.wait()

    def attn_part(o, carry):
        send_a[o] = jnp.dot(mixed[...], wo[:, columns(o)], preferred_element_type=jnp.float32)
        return carry

    lax.fori_loop(0, n, attn_part, 0)
    start_all(axis, n, lambda peer: send_a.at[peer], recv_a, a_sem)
    recv_a[me] = send_a[me]
    recv_all(axis, n, recv_a, a_sem)
    own = recv_a[0]
    for o in range(1, n):
        own = own + recv_a[o]
    own = last_cols[...] + own
    full[me] = own
    start_all(axis, n, lambda peer: full.at[me], full, g_sem)
    recv_all(axis, n, full, g_sem)
    square = full[0] * full[0]
    for o in range(1, n):
        square = square + full[o] * full[o]
    scale = lax.rsqrt(jnp.sum(square, axis=-1, keepdims=True) / width + EPS)
    for o in range(n):
        m_norm[o] = (full[o] * scale * gains[o, 1:2, :]).astype(jnp.bfloat16)

    def widen(o, carry):
        for copy in part_copies(o):
            copy.wait()
        one = m_norm[o]
        gate = jnp.dot(one, wg[columns(o), :], preferred_element_type=jnp.float32)
        up = jnp.dot(one, wu[columns(o), :], preferred_element_type=jnp.float32)
        return (carry[0] + gate, carry[1] + up)

    zero = jnp.zeros((cands, hidden), jnp.float32)
    gate, up = lax.fori_loop(0, n, widen, (zero, zero))
    act = (gate / (1.0 + jnp.exp(-gate)) * up).astype(jnp.bfloat16)
    down_copy.wait()

    def down_part(k, carry):
        o = peer_of(me, k, n)
        send_d[o] = jnp.dot(act, wd[:, columns(o)], preferred_element_type=jnp.float32)

        remote(send_d.at[o], recv_d.at[me], d_sem.at[0, k], d_sem.at[1, k], axis, o).start()
        return carry

    lax.fori_loop(1, n, down_part, 0)
    recv_d[me] = jnp.dot(act, wd[:, columns(me)], preferred_element_type=jnp.float32)
    recv_all(axis, n, recv_d, d_sem)
    mlp = recv_d[0]
    for o in range(1, n):
        mlp = mlp + recv_d[o]
    mlp = full[me] + mlp
    feat = mlp * gain_final[...]
    lane = lax.broadcasted_iota(jnp.int32, (cands, HEAD_DIM), 1)
    stats[me] = jnp.where(
        lane == 0,
        jnp.sum(mlp * mlp, axis=-1, keepdims=True),
        jnp.sum(feat * reward[...], axis=-1, keepdims=True),
    )
    start_all(axis, n, lambda peer: stats.at[me], stats, s_sem)
    recv_all(axis, n, stats, s_sem)
    total = stats[0]
    for o in range(1, n):
        total = total + stats[o]
    scale = lax.rsqrt(total[:, 0:1] / width + EPS)
    feats[judge] = feat * scale
    scores[judge] = total * scale
    start_all("judge", judges, lambda peer: feats.at[judge], feats, f_sem)
    start_all("judge", judges, lambda peer: scores.at[judge], scores, c_sem)
    recv_all("judge", judges, feats, f_sem)
    recv_all("judge", judges, scores, c_sem)
    feat = feats[0]
    score = scores[0]
    for j in range(1, judges):
        feat = feat + feats[j]
        score = score + scores[j]
    feat_out[...] = feat
    score_out[...] = score
    sent_all(axis, n, recv_a, a_sem)
    sent_all(axis, n, full, g_sem)
    sent_all(axis, n, recv_d, d_sem)
    sent_all(axis, n, stats, s_sem)
    sent_all("judge", judges, feats, f_sem)
    sent_all("judge", judges, scores, c_sem)


def body(
    hidden,
    lengths,
    duplicate_group_index,
    attn_gain,
    w_query,
    w_key,
    w_value,
    w_out,
    mlp_gain,
    w_gate,
    w_up,
    w_down,
    final_gain,
    reward_head,
):
    judges = lax.axis_size("judge")
    n = lax.axis_size("fsdp")
    me = lax.axis_index("fsdp")
    tokens = hidden[0]
    tok_dev, width = tokens.shape
    seq_dev = tok_dev // LEN
    cands = lengths.shape[0]
    duplicate_groups = cands // 4
    heads = width // HEAD_DIM
    groups = heads // KV_HEADS
    cols = width // n
    heads_dev = cols // HEAD_DIM
    kvw = w_key.shape[2]
    f32, bf16 = jnp.float32, jnp.bfloat16
    own_len = lax.dynamic_slice_in_dim(lengths, me * seq_dev, seq_dev)
    own_last = jnp.concatenate(
        [
            lax.dynamic_slice_in_dim(tokens, s * LEN + own_len[s] - 1, 1, 0)
            for s in range(seq_dev)
        ],
        axis=0,
    ).astype(f32)
    pack_width = seq_dev * width // 8
    last_pack = own_last.reshape(seq_dev, width // pack_width, pack_width)
    last_pack = last_pack.transpose(1, 0, 2).reshape(8, pack_width)
    gain_pack = jnp.concatenate(
        [attn_gain, mlp_gain, final_gain, jnp.zeros((5, cols), bf16)], axis=0
    ).astype(f32)

    def table(position):
        cosine, sine = angles(position)
        return (
            jnp.concatenate([cosine, cosine], axis=-1),
            jnp.concatenate([-sine, sine], axis=-1),
        )

    q_cos, q_sin = table((lengths - 1).astype(f32))
    k_cos, k_sin = table(jnp.arange(LEN, dtype=f32))
    kpd = max(1, KV_HEADS // n)
    q_rows = max(8, heads_dev * seq_dev)
    each = KV_HEADS * groups
    vmem = pl.BlockSpec(memory_space=pltpu.VMEM)
    anywhere = pl.BlockSpec(memory_space=pl.ANY)
    dma = pltpu.SemaphoreType.DMA
    mixed_pack, x_last, gains = pl.pallas_call(
        functools.partial(attend_kernel, n, seq_dev),
        out_shape=(
            jax.ShapeDtypeStruct((kpd, n, seq_dev * groups, HEAD_DIM), f32),
            jax.ShapeDtypeStruct((cands, width), f32),
            jax.ShapeDtypeStruct((n, 8, cols), f32),
        ),
        in_specs=[pl.BlockSpec(memory_space=pltpu.SMEM)] + [anywhere] * 4 + [vmem] * 6,
        out_specs=(vmem, vmem, vmem),
        scratch_shapes=[
            pltpu.VMEM((n, 2, cols, kvw // 2), bf16),
            pltpu.VMEM((n, tok_dev, cols), bf16),
            pltpu.VMEM((2, tok_dev, kvw // 2), f32),
            pltpu.VMEM((width, cols), bf16),
            pltpu.VMEM((cols, kvw), bf16),
            pltpu.VMEM((2, 128, width), bf16),
            pltpu.VMEM((n, 8, pack_width), f32),
            pltpu.VMEM((n, 8, cols), f32),
            pltpu.VMEM((cands, width), f32),
            pltpu.VMEM((1, width), f32),
            pltpu.VMEM((n, q_rows, HEAD_DIM), f32),
            pltpu.VMEM((n, q_rows, HEAD_DIM), f32),
            pltpu.VMEM((KV_HEADS, seq_dev * groups, HEAD_DIM), f32),
            pltpu.VMEM((seq_dev, heads, LEN), f32),
            pltpu.VMEM((n, seq_dev * each, cols), bf16),
            pltpu.VMEM((n, seq_dev * each, cols), bf16),
            pltpu.VMEM((n, seq_dev * each, kvw), f32),
            pltpu.VMEM((n, kpd, n, seq_dev * groups, HEAD_DIM), f32),
            pltpu.VMEM((n, kpd, n, seq_dev * groups, HEAD_DIM), f32),
            dma((2, 2, n)),
            dma((2, 2, n)),
            dma((4,)),
            dma((2,)),
            dma((2, n)),
            dma((2, n)),
            dma((2, n)),
            dma((2, n)),
            dma((2, n)),
        ],
        compiler_params=pltpu.CompilerParams(
            collective_id=0, has_side_effects=True, vmem_limit_bytes=50 * 2**20
        ),
    )(
        own_len,
        tokens,
        w_query[0],
        w_key[0],
        w_value[0],
        last_pack,
        gain_pack,
        q_cos,
        q_sin,
        k_cos,
        k_sin,
    )
    mixed = mixed_pack.reshape(kpd, n, seq_dev, groups, HEAD_DIM)
    mixed = mixed.transpose(1, 2, 0, 3, 4).reshape(cands, kpd * groups * HEAD_DIM).astype(bf16)
    first = lax.rem(me * heads_dev, groups) if heads_dev < groups else 0
    mixed = lax.dynamic_slice_in_dim(mixed, first * HEAD_DIM, cols, 1)
    last_cols = lax.dynamic_slice_in_dim(x_last, me * cols, cols, 1)
    reward = lax.dynamic_slice_in_dim(reward_head, me * cols, cols, 1)
    hidden_dev = w_gate.shape[2]
    total_cols, score_total = pl.pallas_call(
        functools.partial(feed_kernel, n, judges),
        out_shape=(
            jax.ShapeDtypeStruct((cands, cols), f32),
            jax.ShapeDtypeStruct((cands, HEAD_DIM), f32),
        ),
        in_specs=[vmem] * 5 + [anywhere] * 4,
        out_specs=(vmem, vmem),
        scratch_shapes=[
            pltpu.VMEM((cols, width), bf16),
            pltpu.VMEM((width, hidden_dev), bf16),
            pltpu.VMEM((width, hidden_dev), bf16),
            pltpu.VMEM((hidden_dev, width), bf16),
            pltpu.VMEM((n, cands, cols), f32),
            pltpu.VMEM((n, cands, cols), f32),
            pltpu.VMEM((n, cands, cols), f32),
            pltpu.VMEM((n, cands, cols), bf16),
            pltpu.VMEM((n, cands, cols), f32),
            pltpu.VMEM((n, cands, cols), f32),
            pltpu.VMEM((n, cands, HEAD_DIM), f32),
            pltpu.VMEM((judges, cands, cols), f32),
            pltpu.VMEM((judges, cands, HEAD_DIM), f32),
            dma((2,)),
            dma((n,)),
            dma((n,)),
            dma((2, n)),
            dma((2, n)),
            dma((2, n)),
            dma((2, n)),
            dma((2, judges)),
            dma((2, judges)),
        ],
        compiler_params=pltpu.CompilerParams(
            collective_id=1, has_side_effects=True, vmem_limit_bytes=60 * 2**20
        ),
    )(
        mixed,
        last_cols,
        gains,
        final_gain.astype(f32),
        reward,
        w_out[0],
        w_gate[0],
        w_up[0],
        w_down[0],
    )
    weight_values, panel_member = remaining_candidates(
        score_total[:, 1] / judges, duplicate_group_index, duplicate_groups
    )
    cluster_cols = jnp.dot(
        panel_member.T,
        weight_values[:, None] * (total_cols / judges),
        precision=lax.Precision.HIGHEST,
    )
    return (weight_values, cluster_cols)


def solution(mesh):
    in_specs = (
        P("judge", "fsdp", None),
        P(),
        P(),
        P("judge", "fsdp"),
        P("judge", None, "fsdp"),
        P("judge", "fsdp", None),
        P("judge", "fsdp", None),
        P("judge", "fsdp", None),
        P("judge", "fsdp"),
        P("judge", None, "fsdp"),
        P("judge", None, "fsdp"),
        P("judge", "fsdp", None),
        P("judge", "fsdp"),
        P("judge", None),
    )
    out_specs = (P(), P(None, "fsdp"))
    return jax.shard_map(body, mesh=mesh, in_specs=in_specs, out_specs=out_specs, check_vma=False)
```
